32 devices in a mesh: row: 4 (over y, x), col: 8 (over z, core).
Axes of the slice: x: 2, y: 2, z: 4, core: 2. Of those that a mesh axis runs over, the one named last changes fastest.
Arguments:
- design: bfloat16 [2048, 24576], P('row', 'col'), may hold values from -0.125 to 0.125
- whitener: bfloat16 [4, 512, 512], replicated, as said below
- arc_length: int32 [4], replicated, may hold values from 1 to 512, 1536 in all
- gap_mask: int32 [4, 512], replicated, may hold values 0 or 1
- prior_diag: float32 [24576], replicated, may hold values from 0.5 to 5
Outputs:
- schur_rest: float32 [8, 3072, 24576], P(None, 'row', 'col')
- panel_factor: float32 [8, 3072, 128], P(None, 'row')
The draws below stay inside these ranges and needn't reach their ends.
Inputs may be any that keep to these rules, and one draw needn't show every extreme that they name: `whitener`: each arc's factor is lower triangular with a positive diagonal. `arc_length`: the longest arc has exactly 512 epochs, and the lengths sum to 1536.
All inputs are finite; a program needn't handle non-finite values.
Results may differ from the reference program's by a relative error of at most 0.003.
Values may be sent and summed in bfloat16 or wider, within the bound.
A program may use at most 192 MiB of HBM per device.

```python
import math
import jax
import jax.numpy as jnp
import numpy as np
from jax import lax

NC = 24576
PANEL = 128
ARCS = 4
EPOCHS = 512
OBS = 2048
N_COL = 8


def draw_whitener(key, part):
    key_diag, key_off = jax.random.split(jax.random.fold_in(key, 7))
    diag_part = jax.random.uniform(key_diag, (ARCS, EPOCHS), jnp.float32, 0.7, 1.4)
    off_part = jax.random.normal(key_off, (ARCS, EPOCHS, EPOCHS), jnp.float32)
    lower_mask = jnp.tril(jnp.ones((EPOCHS, EPOCHS), jnp.float32), -1)
    scaled = off_part * lower_mask[None] * EPOCHS ** (-0.5)
    eye_table = jnp.eye(EPOCHS, dtype=jnp.float32)
    return (scaled + diag_part[:, :, None] * eye_table[None]).astype(jnp.bfloat16)


def with_ends(result, key, smallest, largest):
    spot = [jax.random.randint(jax.random.fold_in(key, axis), (), 0, length) for axis, length in enumerate(result.shape)]
    widest = result.shape.index(max(result.shape))
    neighbour = spot[:widest] + [(spot[widest] + 1) % result.shape[widest]] + spot[widest + 1:]
    return result.at[tuple(spot)].set(smallest).at[tuple(neighbour)].set(largest)


def block_scale(stream_key, shape, shards, smallest, top_value):
    loudness = 1.0
    for dim, parts in shards:
        steps = jax.random.uniform(jax.random.fold_in(jax.random.fold_in(stream_key, 6), dim), (parts,), jnp.float32, smallest / len(shards), top_value / len(shards))
        loudness = loudness * jnp.repeat(jnp.exp(steps), shape[dim] // parts).reshape((-1,) + (1,) * (len(shape) - 1 - dim))
    return loudness


def profile(amount, total, most, skew):
    portions = [(1 << 20) // math.isqrt(rank ** skew) + 1 for rank in range(2, amount + 1)]
    rest, counts = total - most - (amount - 1), [1] * (amount - 1)
    while rest > 0:
        candidates = [i for i in range(amount - 1) if counts[i] < most]
        mass, budget = sum([portions[i] for i in candidates]), rest
        for i in candidates:
            addition = min(most - counts[i], max(1, budget * portions[i] // mass), rest)
            counts[i] = counts[i] + addition
            rest = rest - addition
    return np.array([most] + counts)


def uneven(key, amount, total, limit, slope):
    if amount == 2:
        one = jax.random.randint(key, (), max(1, total - limit), min(limit, total - 1) + 1)
        return jnp.stack([one, total - one])
    lengths = jnp.asarray(profile(amount, total, limit, slope), jnp.int32)
    twos = (amount - 1) // 2
    giver, taker = lengths[1:1 + 2 * twos:2], lengths[2:2 + 2 * twos:2]
    slack = jnp.minimum(giver - 1, limit - taker)
    moved = jax.random.randint(jax.random.fold_in(key, 1), (twos,), 0, 1 << 20) % (slack + 1)
    lengths = lengths.at[1:1 + 2 * twos:2].set(giver - moved).at[2:2 + 2 * twos:2].set(taker + moved)
    return lengths[jax.random.permutation(jax.random.fold_in(key, 2), amount)]


def scatter_about(own_key, dims, deviation, most, pieces=(), held_as=jnp.bfloat16):
    drawn = jax.random.normal(own_key, dims, jnp.float32) * deviation
    if len(pieces) > 0:
        drawn = block_scale(own_key, dims, pieces, -0.22, 0.18) * drawn
    return jnp.clip(drawn, min=-most, max=most).astype(held_as)


def setup_inputs(seed: int = 0) -> dict:
    keys = jax.random.split(jax.random.key(seed), 6)
    design = scatter_about(keys[0], (OBS, NC), (ARCS * EPOCHS) ** -0.5, 0.125, ((0, 4), (1, 8)))
    whitener = draw_whitener(jax.random.fold_in(keys[5], 71), 0)
    arc_length = uneven(keys[2], ARCS, 3 * EPOCHS, EPOCHS, 2).astype(jnp.int32)
    gap_mask = with_ends((jax.random.randint(keys[3], (ARCS, EPOCHS), 0, 4) < 3).astype(jnp.int32), jax.random.fold_in(keys[3], 1), 0, 1)
    prior_diag = jnp.clip(jnp.exp(jax.random.uniform(keys[4], (NC,), jnp.float32, math.log(0.5), math.log(5.0))), 0.5, 5.0)
    return {"design": design, "whitener": whitener, "arc_length": arc_length, "gap_mask": gap_mask, "prior_diag": prior_diag}


def live_mask(arc_length, gap_mask):
    epoch_ids = lax.broadcasted_iota(jnp.int32, gap_mask.shape, 1)
    keep_epoch = (epoch_ids < arc_length[:, None].astype(jnp.int32)) & (gap_mask == 1)
    return jnp.where(keep_epoch, jnp.float32(1.0), jnp.float32(0.0))

def reference(design, whitener, arc_length, gap_mask, prior_diag):
    weights = live_mask(arc_length, gap_mask)
    shaped = design.astype(jnp.float32).reshape(ARCS, EPOCHS, NC) * weights[:, :, None]
    mixed_rows = jnp.einsum('aij,ajk->aik', whitener.astype(jnp.float32), shaped, precision=lax.Precision.HIGHEST)
    whitened = (mixed_rows * weights[:, :, None]).astype(jnp.bfloat16).reshape(ARCS * EPOCHS, NC)
    white_wide = whitened.astype(jnp.float32)
    normal = lax.dot_general(white_wide, white_wide, (((0,), (0,)), ((), ())), precision=lax.Precision.HIGHEST)
    diag_ids = jnp.arange(NC, dtype=jnp.int32)
    normal = normal.at[diag_ids, diag_ids].add(prior_diag)
    factor = jnp.linalg.cholesky(normal[:PANEL, :PANEL])
    panel_out = lax.linalg.triangular_solve(factor, normal[:, :PANEL], left_side=False, lower=True, transpose_a=True)
    row_block = NC // N_COL

    def update(step_index, matrix):
        offset = (step_index * row_block).astype(jnp.int32)
        row_slab = lax.dynamic_slice_in_dim(matrix, offset, row_block, 0)
        left_slab = lax.dynamic_slice_in_dim(panel_out, offset, row_block, 0)
        row_slab = row_slab - jnp.dot(left_slab, panel_out.T, precision=lax.Precision.HIGHEST)
        return lax.dynamic_update_slice_in_dim(matrix, row_slab, offset, 0)
    schur = lax.fori_loop(0, N_COL, update, normal)
    return (schur.reshape(N_COL, NC // N_COL, NC), panel_out.reshape(N_COL, NC // N_COL, PANEL))
```

```python
import functools

import jax
import jax.numpy as jnp
import numpy as np
from jax import lax
from jax.experimental import pallas as pl
from jax.experimental.pallas import tpu as pltpu
from jax.sharding import PartitionSpec as P

PANEL = 128
LANES = 128
F32 = jnp.float32
BF16 = jnp.bfloat16
EXACT = lax.Precision.HIGHEST


def params(**more):
    return pltpu.CompilerParams(vmem_limit_bytes=48 * 2**20, **more)


def cost(flops, nbytes):
    return pl.CostEstimate(flops=int(flops), bytes_accessed=int(nbytes), transcendentals=0)


def iota(shape, dim):
    return lax.broadcasted_iota(jnp.int32, shape, dim)


def split_two(value):
    high = value.astype(BF16)
    return high, (value - high.astype(F32)).astype(BF16)


def live_mask(arc_length, gap_mask):
    return (iota(gap_mask.shape, 1) < arc_length[:, None]) & (gap_mask == 1)


def compact_whitener(whitener, live, kept):
    arcs, epochs = live.shape
    flat = live.reshape(-1)
    place = (jnp.cumsum(flat.astype(jnp.int32)) - 1).reshape(arcs, 1, epochs)
    pick = (iota((arcs, kept, epochs), 1) == place) & live[:, None, :]
    rows = jnp.einsum("ake,aef->akf", pick.astype(BF16), whitener, preferred_element_type=F32)
    return jnp.where(live[:, None, :], rows, 0.0).astype(BF16)


def whiten_kernel(order_ref, mixer_ref, *refs):
    blocks, out_ref = refs[:-1], refs[-1]
    total = jnp.dot(mixer_ref[order_ref[0]], blocks[0][...], preferred_element_type=F32)
    for s in range(1, len(blocks)):
        total += jnp.dot(mixer_ref[order_ref[s]], blocks[s][...], preferred_element_type=F32)
    out_ref[...] = total.astype(BF16)


def whiten(order, mixer, blocks):
    arcs, kept, epochs = mixer.shape
    width = blocks[0].shape[1]
    part = kept // 2
    return pl.pallas_call(
        whiten_kernel,
        grid_spec=pltpu.PrefetchScalarGridSpec(
            num_scalar_prefetch=1,
            grid=(2,),
            in_specs=[pl.BlockSpec((arcs, part, epochs), lambda i, o: (0, i, 0))]
            + [pl.BlockSpec(b.shape, lambda i, o: (0, 0)) for b in blocks],
            out_specs=pl.BlockSpec((part, width), lambda i, o: (i, 0)),
        ),
        out_shape=jax.ShapeDtypeStruct((kept, width), BF16),
        compiler_params=params(),
        cost_estimate=cost(2 * kept * arcs * epochs * width, 2 * arcs * epochs * (kept + width)),
        name="whiten",
    )(order, mixer, *blocks)


def factor_kernel(first_ref, prior_ref, inv_ref, inv_t_ref):
    first = first_ref[...]
    n = first.shape[1]
    same = iota((n, n), 0) == iota((n, n), 1)
    corner = jnp.dot(first.T, first, preferred_element_type=F32)
    corner = corner + jnp.where(same, prior_ref[...], 0.0)
    rows, lanes = iota((n, n), 0), iota((n, n), 1)
    row_ids = iota((n, 1), 0)

    def step(k, held):
        a, r = held
        at_row = rows == k
        a_row = jnp.sum(jnp.where(at_row, a, 0.0), axis=0, keepdims=True)
        r_row = jnp.sum(jnp.where(at_row, r, 0.0), axis=0, keepdims=True)
        column = jnp.sum(jnp.where(lanes == k, a, 0.0), axis=1, keepdims=True)
        pivot = jnp.sum(jnp.where(lanes[:1] == k, a_row, 0.0), axis=1, keepdims=True)
        share = jnp.where(row_ids > k, column / pivot, 0.0)
        return a - share * a_row, r - share * r_row

    a, r = lax.fori_loop(0, n, step, (corner, jnp.where(same, 1.0, 0.0).astype(F32)))
    diagonal = jnp.sum(jnp.where(same, a, 0.0), axis=1, keepdims=True)
    inverse = r / jnp.sqrt(diagonal)
    inv_ref[...] = inverse
    inv_t_ref[...] = inverse.T


def factor_inverse(first, prior):
    n = first.shape[1]
    square = jax.ShapeDtypeStruct((n, n), F32)
    return pl.pallas_call(
        factor_kernel,
        out_shape=(square, square),
        compiler_params=params(),
        cost_estimate=cost(2e10, 2 * first.size),
        name="factor_inverse",
    )(first, prior)


def right_kernel(kept, count, where_ref, first_ref, prior_ref, inv_ref, *refs):
    parts, out_ref = refs[:count], refs[-1]
    strip = jnp.concatenate([p[...] for p in parts], axis=0) if count > 1 else parts[0][...]
    rows, width = strip.shape
    n = first_ref.shape[1]
    top = jnp.dot(first_ref[...].T, strip, preferred_element_type=F32)
    same = (iota((n, width), 0) == iota((n, width), 1)) & (where_ref[0] == 0)
    top = top + jnp.where(same, prior_ref[...], 0.0)
    solved = jnp.dot(inv_ref[...], top, precision=EXACT, preferred_element_type=F32)
    high, low = split_two(solved)
    out_ref[0, :rows] = strip
    if kept > rows:
        out_ref[0, rows:kept] = jnp.zeros((kept - rows, width), BF16)
    out_ref[0, kept : kept + n] = high
    out_ref[0, kept + n : kept + 2 * n] = low
    out_ref[0, kept + 2 * n :] = high


def right_side(kept, slot, slots, column, first, prior, inverse, parts, held):
    width = parts[0].shape[1]
    n = first.shape[1]
    depth = kept + 3 * n
    whole = lambda a: pl.BlockSpec(a.shape, lambda i, w: (0,) * a.ndim)
    operands = [first, prior, inverse] + list(parts)
    specs = [whole(a) for a in operands]
    aliases = {}
    if held is not None:
        aliases = {1 + len(operands): 0}
        operands.append(held)
        specs.append(pl.BlockSpec(memory_space=pl.ANY))
    return pl.pallas_call(
        functools.partial(right_kernel, kept, len(parts)),
        grid_spec=pltpu.PrefetchScalarGridSpec(
            num_scalar_prefetch=1,
            grid=(1,),
            in_specs=specs,
            out_specs=pl.BlockSpec((1, depth, width), lambda i, w: (slot, 0, 0)),
        ),
        out_shape=jax.ShapeDtypeStruct((slots, depth, width), BF16),
        input_output_aliases=aliases,
        compiler_params=params(),
        cost_estimate=cost(2 * n * width * (kept + 6 * n), 4 * depth * width),
        name="right_side",
    )(column, *operands)


def tile_kernel(kept, choices, at_ref, order_ref, *refs):
    candidates = [refs[2 * q : 2 * q + 2] for q in range(choices)]
    refs = refs[2 * choices :]
    right_ref, first_ref, prior_ref, first_prior_ref, inv_t_ref = refs[:5]
    schur_ref, panel_ref, landed, left, sems = refs[-5:]
    s, i = pl.program_id(0), pl.program_id(1)
    rows = candidates[0][0].shape[0]
    width = left.shape[1]
    n = first_ref.shape[1]
    block = at_ref[0] * 2 + (i ^ at_ref[4])
    row_index, col_index, choice = at_ref[1], at_ref[2], at_ref[3]

    @pl.when((s == 0) & (i == 0))
    def _():
        if kept > rows:
            for g in range(2):
                landed[g, rows:kept] = jnp.zeros((kept - rows, width), BF16)
        for q in range(choices):

            @pl.when(choice == q)
            def _():
                for g in range(2):
                    pltpu.make_async_copy(
                        candidates[q][g], landed.at[g, pl.ds(0, rows)], sems.at[g]
                    ).start()

    @pl.when(s == 0)
    def _():
        pltpu.make_async_copy(
            candidates[0][0], landed.at[i, pl.ds(0, rows)], sems.at[i]
        ).wait()
        turned = landed[i].T
        left[i, :, :kept] = turned
        near = jnp.dot(turned, first_ref[...], preferred_element_type=F32)
        same = (iota((width, n), 0) == iota((width, n), 1)) & (block + row_index == 0)
        near = near + jnp.where(same, first_prior_ref[...], 0.0)
        solved = jnp.dot(near, inv_t_ref[...], precision=EXACT, preferred_element_type=F32)
        panel_ref[0] = solved
        high, low = split_two(-solved)
        left[i, :, kept : kept + n] = high
        left[i, :, kept + n : kept + 2 * n] = high
        left[i, :, kept + 2 * n :] = low

    schur_ref[0] = jnp.dot(left[i], right_ref[0], preferred_element_type=F32)

    @pl.when((block == col_index) & (s == 0))
    def _():
        same = iota((width, width), 0) == iota((width, width), 1)
        schur_ref[0] = schur_ref[0] + jnp.where(same, prior_ref[...], 0.0)


def tiles(kept, at, order, pairs, right, first, prior, first_prior, inv_t, blocks, held):
    slots, depth, width = right.shape
    rows = pairs[0][0].shape[0]
    n = first.shape[1]
    whole = lambda a: pl.BlockSpec(a.shape, lambda s, i, at, order: (0,) * a.ndim)
    anywhere = pl.BlockSpec(memory_space=pl.ANY)
    operands = [half for pair in pairs for half in pair]
    specs = [anywhere] * len(operands)
    operands += [right, first, prior, first_prior, inv_t]
    specs += [pl.BlockSpec((1, depth, width), lambda s, i, at, order: (s, 0, 0))]
    specs += [whole(a) for a in operands[-4:]]
    aliases = {}
    if held is not None:
        aliases = {2 + len(operands): 0, 3 + len(operands): 1}
        operands += list(held)
        specs += [anywhere] * 2
    return pl.pallas_call(
        functools.partial(tile_kernel, kept, len(pairs)),
        grid_spec=pltpu.PrefetchScalarGridSpec(
            num_scalar_prefetch=2,
            grid=(slots, 2),
            in_specs=specs,
            out_specs=[
                pl.BlockSpec(
                    (1, width, width),
                    lambda s, i, at, order: (at[0] * 2 + (i ^ at[4]), 0, order[s]),
                ),
                pl.BlockSpec(
                    (1, width, n),
                    lambda s, i, at, order: (at[0] * 2 + (jnp.where(s == 0, i, 1) ^ at[4]), 0, 0),
                ),
            ],
            scratch_shapes=[
                pltpu.VMEM((2, kept, width), BF16),
                pltpu.VMEM((2, width, depth), BF16),
                pltpu.SemaphoreType.DMA((2,)),
            ],
        ),
        out_shape=(
            jax.ShapeDtypeStruct((blocks, width, slots * width), F32),
            jax.ShapeDtypeStruct((blocks, width, n), F32),
        ),
        input_output_aliases=aliases,
        compiler_params=params(),
        cost_estimate=cost(
            4 * width * width * slots * depth, 8 * width * width * slots + 2 * right.size
        ),
        name="tiles",
    )(at, order, *operands)


def line_schedule(chips):
    table = []
    for z in range(chips):
        others = [(abs(q - z), int(q > z), q) for q in range(chips) if q != z]
        table.append([(q, side, d) for d, side, q in sorted(others)])
    return table


def broadcast(value, axis, root):
    mine = lax.axis_index(axis) == root
    return lax.psum(jnp.where(mine, value, jnp.zeros_like(value)), axis)


def whiten_rows(design_rows, whitener, weights):
    arc_count, epoch_count = weights.shape
    shaped = design_rows.reshape(arc_count, epoch_count, design_rows.shape[1])
    masked = shaped * weights[:, :, None].astype(jnp.bfloat16)
    mixed_rows = jnp.einsum("aij,ajk->aik", whitener, masked, preferred_element_type=jnp.float32)
    return (mixed_rows * weights[:, :, None]).astype(jnp.bfloat16).reshape(design_rows.shape)


def contract_rows(left_side, right_side):
    return lax.dot_general(
        left_side, right_side, (((0,), (0,)), ((), ())), preferred_element_type=jnp.float32
    )


def add_prior(matrix, row_ids, column_ids, column_prior):
    return matrix + jnp.where(
        row_ids[:, None] == column_ids[None, :], column_prior[None, :], jnp.float32(0.0)
    )


def by_blocks(design, whitener, arc_length, gap_mask, prior_diag):
    weights = jnp.where(live_mask(arc_length, gap_mask), jnp.float32(1.0), jnp.float32(0.0))
    row_index = lax.axis_index("row")
    col_index = lax.axis_index("col")
    row_count = lax.axis_size("row")
    col_count = lax.axis_size("col")
    col_width = design.shape[1]
    strip_width = col_width // row_count
    regrouped = lax.all_to_all(design, "row", split_axis=1, concat_axis=0, tiled=True)
    own_strip = whiten_rows(regrouped, whitener, weights)
    column_side = lax.all_gather(own_strip, "row", axis=1, tiled=True)
    column_ids = col_index * col_width + lax.broadcasted_iota(jnp.int32, (col_width,), 0)
    column_prior = lax.dynamic_slice_in_dim(prior_diag, col_index * col_width, col_width)
    first_ids = lax.broadcasted_iota(jnp.int32, (PANEL,), 0)
    block_ids = lax.broadcasted_iota(jnp.int32, (col_count, strip_width), 0) * col_width
    block_ids = (
        block_ids
        + row_index * strip_width
        + lax.broadcasted_iota(jnp.int32, (col_count, strip_width), 1)
    ).reshape(-1)
    first_white = broadcast(own_strip[:, :PANEL], ("row", "col"), 0)
    top_rows = add_prior(
        contract_rows(first_white, column_side), first_ids, column_ids, column_prior
    )
    corner = add_prior(
        contract_rows(first_white, first_white), first_ids, first_ids, prior_diag[:PANEL]
    )
    section = lax.all_gather(own_strip, "col", axis=1, tiled=True)
    wide_tile = jnp.concatenate(
        [contract_rows(section, column_side), contract_rows(section, first_white)], axis=1
    )
    normal_tile = add_prior(wide_tile[:, :col_width], block_ids, column_ids, column_prior)
    panel_cols = add_prior(wide_tile[:, col_width:], block_ids, first_ids, prior_diag[:PANEL])
    factor = jnp.linalg.cholesky(corner)
    panel_left = lax.linalg.triangular_solve(
        factor, panel_cols, left_side=False, lower=True, transpose_a=True
    )
    panel_top = lax.linalg.triangular_solve(factor, top_rows, left_side=True, lower=True)
    schur = normal_tile - jnp.dot(
        panel_left, panel_top, precision=lax.Precision.HIGHEST, preferred_element_type=jnp.float32
    )
    return (
        schur.reshape(col_count, strip_width, col_width),
        panel_left.reshape(col_count, strip_width, PANEL),
    )


def on_device(design, whitener, arc_length, gap_mask, prior_diag):
    live = live_mask(arc_length, gap_mask)
    row_index = lax.axis_index("row")
    col_index = lax.axis_index("col")
    rows = lax.axis_size("row")
    cols = lax.axis_size("col")
    chips = cols // 2
    arcs, epochs = live.shape
    col_width = design.shape[1]
    width = col_width // rows
    chip = col_index // 2
    order = row_index ^ jnp.arange(rows, dtype=jnp.int32)

    def swap_row(value, mask):
        return lax.ppermute(value, "row", [(r, r ^ mask) for r in range(rows)])

    def swap_core(value):
        return lax.ppermute(value, "col", [(c, c ^ 1) for c in range(cols)])

    def shift(value, step):
        pairs = [(c, c + 2 * step) for c in range(cols) if 0 <= c + 2 * step < cols]
        return lax.ppermute(value, "col", pairs)

    def strip_of(index):
        return lax.dynamic_slice_in_dim(design, index * width, width, axis=1)

    raw = [strip_of(row_index)]
    for s in range(1, rows):
        raw.append(swap_row(strip_of(row_index ^ s), s))

    column_prior = lax.dynamic_slice_in_dim(
        prior_diag, col_index * col_width + row_index * width, width
    ).reshape(1, width)
    first_prior = prior_diag[:PANEL]
    table = line_schedule(chips)

    def run(sent, raw):
        kept = -(-sent // LANES) * LANES
        own = whiten(order, compact_whitener(whitener, live, sent), raw)

        mine = (row_index == 0) & (col_index == 0)
        first = jnp.where(mine, own[:, :PANEL], jnp.zeros((sent, PANEL), BF16))
        first = lax.psum(first, ("row", "col"))

        moving = {0: own, 1: own}
        arrived = {}
        for t in range(1, chips):
            moving = {0: shift(moving[0], 1), 1: shift(moving[1], -1)}
            arrived[0, t], arrived[1, t] = moving[0], moving[1]

        core = col_index % 2

        near = [own] + [swap_row(own, 1 << b) for b in range((rows - 1).bit_length())]
        half = sent // 32 * 16
        strips = {0: [own], 1: [near[1]], 2: [near[2]]}
        strips[3] = [swap_row(near[2][:half], 1), swap_row(near[1][half:], 2)]

        inverse, inv_t = factor_inverse(first, first_prior.reshape(1, PANEL))
        wide = jnp.pad(first, ((0, kept - sent), (0, 0)))
        top_prior = first_prior.reshape(PANEL, 1)
        right = None
        for s in range(rows):
            spot = (col_index + (row_index ^ s)).reshape(1)
            right = right_side(
                kept, s, rows, spot, first, top_prior, inverse, strips[s], right
            )

        held = None
        sibling = {0: swap_core(own)}
        for key, value in arrived.items():
            sibling[key] = swap_core(value)
        for t in range(chips):
            if t == 0:
                keys, target, choice = [0], chip, jnp.int32(0)
                source = {0: own}
            else:
                wanted = [table[z][t - 1] for z in range(chips)]
                keys = sorted({(side, d) for _, side, d in wanted})
                target = jnp.asarray(np.array([q for q, _, _ in wanted], np.int32))[chip]
                choice = jnp.asarray(
                    np.array([keys.index((side, d)) for _, side, d in wanted], np.int32)
                )[chip]
                source = arrived
            pairs = [(source[k], sibling[k]) for k in keys]
            at = jnp.stack([target, row_index, col_index, choice, core]).astype(jnp.int32)
            held = tiles(
                kept, at, order, pairs, right, wide, column_prior,
                first_prior.reshape(1, PANEL), inv_t, cols, held,
            )
        return held

    most = 3 * epochs
    sizes = [most * 19 // 24, most]
    count = jnp.sum(live.astype(jnp.int32))
    return lax.switch(
        jnp.where(count <= sizes[0], 0, 1),
        [functools.partial(run, size) for size in sizes],
        raw,
    )


def solution(mesh):
    def run(design, whitener, arc_length, gap_mask, prior_diag):
        rows = lax.axis_size("row")
        fits = rows == 4 and whitener.shape[0] == rows and design.shape[1] % (rows * LANES) == 0
        form = on_device if fits else by_blocks
        return form(design, whitener, arc_length, gap_mask, prior_diag)

    placed = (P("row", "col"), P(), P(), P(), P())
    return jax.shard_map(
        run,
        mesh=mesh,
        in_specs=placed,
        out_specs=(P(None, "row", "col"), P(None, "row", None)),
        check_vma=False,
    )
```

```python
import functools

import jax
import jax.numpy as jnp
import numpy as np
from jax import lax
from jax.experimental import pallas as pl
from jax.experimental.pallas import tpu as pltpu
from jax.sharding import PartitionSpec as P

PANEL = 128
LANES = 128
F32 = jnp.float32
BF16 = jnp.bfloat16
EXACT = lax.Precision.HIGHEST


def params(**more):
    return pltpu.CompilerParams(vmem_limit_bytes=48 * 2**20, **more)


def cost(flops, nbytes):
    return pl.CostEstimate(flops=int(flops), bytes_accessed=int(nbytes), transcendentals=0)


def iota(shape, dim):
    return lax.broadcasted_iota(jnp.int32, shape, dim)


def split_two(value):
    high = value.astype(BF16)
    return high, (value - high.astype(F32)).astype(BF16)


def live_mask(arc_length, gap_mask):
    return (iota(gap_mask.shape, 1) < arc_length[:, None]) & (gap_mask == 1)


def compact_whitener(whitener, live, kept):
    arcs, epochs = live.shape
    flat = live.reshape(-1)
    place = (jnp.cumsum(flat.astype(jnp.int32)) - 1).reshape(arcs, 1, epochs)
    pick = (iota((arcs, kept, epochs), 1) == place) & live[:, None, :]
    rows = jnp.einsum("ake,aef->akf", pick.astype(BF16), whitener, preferred_element_type=F32)
    return jnp.where(live[:, None, :], rows, 0.0).astype(BF16)


def whiten_kernel(order_ref, mixer_ref, *refs):
    blocks, out_ref = refs[:-1], refs[-1]
    total = jnp.dot(mixer_ref[order_ref[0]], blocks[0][...], preferred_element_type=F32)
    for s in range(1, len(blocks)):
        total += jnp.dot(mixer_ref[order_ref[s]], blocks[s][...], preferred_element_type=F32)
    out_ref[...] = total.astype(BF16)


def whiten(order, mixer, blocks):
    arcs, kept, epochs = mixer.shape
    width = blocks[0].shape[1]
    part = kept // 2
    return pl.pallas_call(
        whiten_kernel,
        grid_spec=pltpu.PrefetchScalarGridSpec(
            num_scalar_prefetch=1,
            grid=(2,),
            in_specs=[pl.BlockSpec((arcs, part, epochs), lambda i, o: (0, i, 0))]
            + [pl.BlockSpec(b.shape, lambda i, o: (0, 0)) for b in blocks],
            out_specs=pl.BlockSpec((part, width), lambda i, o: (i, 0)),
        ),
        out_shape=jax.ShapeDtypeStruct((kept, width), BF16),
        compiler_params=params(),
        cost_estimate=cost(2 * kept * arcs * epochs * width, 2 * arcs * epochs * (kept + width)),
        name="whiten",
    )(order, mixer, *blocks)


def factor_kernel(first_ref, prior_ref, inv_ref, inv_t_ref):
    first = first_ref[...]
    n = first.shape[1]
    same = iota((n, n), 0) == iota((n, n), 1)
    corner = jnp.dot(first.T, first, preferred_element_type=F32)
    corner = corner + jnp.where(same, prior_ref[...], 0.0)
    rows, lanes = iota((n, n), 0), iota((n, n), 1)
    row_ids = iota((n, 1), 0)

    def step(k, held):
        a, r = held
        at_row = rows == k
        a_row = jnp.sum(jnp.where(at_row, a, 0.0), axis=0, keepdims=True)
        r_row = jnp.sum(jnp.where(at_row, r, 0.0), axis=0, keepdims=True)
        column = jnp.sum(jnp.where(lanes == k, a, 0.0), axis=1, keepdims=True)
        pivot = jnp.sum(jnp.where(lanes[:1] == k, a_row, 0.0), axis=1, keepdims=True)
        share = jnp.where(row_ids > k, column / pivot, 0.0)
        return a - share * a_row, r - share * r_row

    a, r = lax.fori_loop(0, n, step, (corner, jnp.where(same, 1.0, 0.0).astype(F32)))
    diagonal = jnp.sum(jnp.where(same, a, 0.0), axis=1, keepdims=True)
    inverse = r / jnp.sqrt(diagonal)
    inv_ref[...] = inverse
    inv_t_ref[...] = inverse.T


def factor_inverse(first, prior):
    n = first.shape[1]
    square = jax.ShapeDtypeStruct((n, n), F32)
    return pl.pallas_call(
        factor_kernel,
        out_shape=(square, square),
        compiler_params=params(),
        cost_estimate=cost(2e10, 2 * first.size),
        name="factor_inverse",
    )(first, prior)


def right_kernel(kept, count, where_ref, first_ref, prior_ref, inv_ref, *refs):
    parts, out_ref = refs[:count], refs[-1]
    strip = jnp.concatenate([p[...] for p in parts], axis=0) if count > 1 else parts[0][...]
    rows, width = strip.shape
    n = first_ref.shape[1]
    top = jnp.dot(first_ref[...].T, strip, preferred_element_type=F32)
    same = (iota((n, width), 0) == iota((n, width), 1)) & (where_ref[0] == 0)
    top = top + jnp.where(same, prior_ref[...], 0.0)
    solved = jnp.dot(inv_ref[...], top, precision=EXACT, preferred_element_type=F32)
    high, low = split_two(solved)
    out_ref[0, :rows] = strip
    if kept > rows:
        out_ref[0, rows:kept] = jnp.zeros((kept - rows, width), BF16)
    out_ref[0, kept : kept + n] = high
    out_ref[0, kept + n : kept + 2 * n] = low
    out_ref[0, kept + 2 * n :] = high


def right_side(kept, slot, slots, column, first, prior, inverse, parts, held):
    width = parts[0].shape[1]
    n = first.shape[1]
    depth = kept + 3 * n
    whole = lambda a: pl.BlockSpec(a.shape, lambda i, w: (0,) * a.ndim)
    operands = [first, prior, inverse] + list(parts)
    specs = [whole(a) for a in operands]
    aliases = {}
    if held is not None:
        aliases = {1 + len(operands): 0}
        operands.append(held)
        specs.append(pl.BlockSpec(memory_space=pl.ANY))
    return pl.pallas_call(
        functools.partial(right_kernel, kept, len(parts)),
        grid_spec=pltpu.PrefetchScalarGridSpec(
            num_scalar_prefetch=1,
            grid=(1,),
            in_specs=specs,
            out_specs=pl.BlockSpec((1, depth, width), lambda i, w: (slot, 0, 0)),
        ),
        out_shape=jax.ShapeDtypeStruct((slots, depth, width), BF16),
        input_output_aliases=aliases,
        compiler_params=params(),
        cost_estimate=cost(2 * n * width * (kept + 6 * n), 4 * depth * width),
        name="right_side",
    )(column, *operands)


def tile_kernel(kept, choices, at_ref, order_ref, *refs):
    candidates = [refs[2 * q : 2 * q + 2] for q in range(choices)]
    refs = refs[2 * choices :]
    right_ref, first_ref, prior_ref, first_prior_ref, inv_t_ref = refs[:5]
    schur_ref, panel_ref, landed, left, sems = refs[-5:]
    s, i = pl.program_id(0), pl.program_id(1)
    rows = candidates[0][0].shape[0]
    width = left.shape[1]
    n = first_ref.shape[1]
    block = at_ref[0] * 2 + (i ^ at_ref[4])
    row_index, col_index, choice = at_ref[1], at_ref[2], at_ref[3]

    @pl.when((s == 0) & (i == 0))
    def _():
        if kept > rows:
            for g in range(2):
                landed[g, rows:kept] = jnp.zeros((kept - rows, width), BF16)
        for q in range(choices):

            @pl.when(choice == q)
            def _():
                for g in range(2):
                    pltpu.make_async_copy(
                        candidates[q][g], landed.at[g, pl.ds(0, rows)], sems.at[g]
                    ).start()

    @pl.when(s == 0)
    def _():
        pltpu.make_async_copy(
            candidates[0][0], landed.at[i, pl.ds(0, rows)], sems.at[i]
        ).wait()
        turned = landed[i].T
        left[i, :, :kept] = turned
        near = jnp.dot(turned, first_ref[...], preferred_element_type=F32)
        same = (iota((width, n), 0) == iota((width, n), 1)) & (block + row_index == 0)
        near = near + jnp.where(same, first_prior_ref[...], 0.0)
        solved = jnp.dot(near, inv_t_ref[...], precision=EXACT, preferred_element_type=F32)
        panel_ref[0] = solved
        high, low = split_two(-solved)
        left[i, :, kept : kept + n] = high
        left[i, :, kept + n : kept + 2 * n] = high
        left[i, :, kept + 2 * n :] = low

    schur_ref[0] = jnp.dot(left[i], right_ref[0], preferred_element_type=F32)

    @pl.when((block == col_index) & (s == 0))
    def _():
        same = iota((width, width), 0) == iota((width, width), 1)
        schur_ref[0] = schur_ref[0] + jnp.where(same, prior_ref[...], 0.0)


def tiles(kept, at, order, pairs, right, first, prior, first_prior, inv_t, blocks, held):
    slots, depth, width = right.shape
    rows = pairs[0][0].shape[0]
    n = first.shape[1]
    whole = lambda a: pl.BlockSpec(a.shape, lambda s, i, at, order: (0,) * a.ndim)
    anywhere = pl.BlockSpec(memory_space=pl.ANY)
    operands = [half for pair in pairs for half in pair]
    specs = [anywhere] * len(operands)
    operands += [right, first, prior, first_prior, inv_t]
    specs += [pl.BlockSpec((1, depth, width), lambda s, i, at, order: (s, 0, 0))]
    specs += [whole(a) for a in operands[-4:]]
    aliases = {}
    if held is not None:
        aliases = {2 + len(operands): 0, 3 + len(operands): 1}
        operands += list(held)
        specs += [anywhere] * 2
    return pl.pallas_call(
        functools.partial(tile_kernel, kept, len(pairs)),
        grid_spec=pltpu.PrefetchScalarGridSpec(
            num_scalar_prefetch=2,
            grid=(slots, 2),
            in_specs=specs,
            out_specs=[
                pl.BlockSpec(
                    (1, width, width),
                    lambda s, i, at, order: (at[0] * 2 + (i ^ at[4]), 0, order[s]),
                ),
                pl.BlockSpec(
                    (1, width, n),
                    lambda s, i, at, order: (at[0] * 2 + (jnp.where(s == 0, i, 1) ^ at[4]), 0, 0),
                ),
            ],
            scratch_shapes=[
                pltpu.VMEM((2, kept, width), BF16),
                pltpu.VMEM((2, width, depth), BF16),
                pltpu.SemaphoreType.DMA((2,)),
            ],
        ),
        out_shape=(
            jax.ShapeDtypeStruct((blocks, width, slots * width), F32),
            jax.ShapeDtypeStruct((blocks, width, n), F32),
        ),
        input_output_aliases=aliases,
        compiler_params=params(),
        cost_estimate=cost(
            4 * width * width * slots * depth, 8 * width * width * slots + 2 * right.size
        ),
        name="tiles",
    )(at, order, *operands)


def line_schedule(chips):
    table = []
    for z in range(chips):
        others = [(abs(q - z), int(q > z), q) for q in range(chips) if q != z]
        table.append([(q, side, d) for d, side, q in sorted(others)])
    return table


def broadcast(value, axis, root):
    mine = lax.axis_index(axis) == root
    return lax.psum(jnp.where(mine, value, jnp.zeros_like(value)), axis)


def whiten_rows(design_rows, whitener, weights):
    arc_count, epoch_count = weights.shape
    shaped = design_rows.reshape(arc_count, epoch_count, design_rows.shape[1])
    masked = shaped * weights[:, :, None].astype(jnp.bfloat16)
    mixed_rows = jnp.einsum("aij,ajk->aik", whitener, masked, preferred_element_type=jnp.float32)
    return (mixed_rows * weights[:, :, None]).astype(jnp.bfloat16).reshape(design_rows.shape)


def contract_rows(left_side, right_side):
    return lax.dot_general(
        left_side, right_side, (((0,), (0,)), ((), ())), preferred_element_type=jnp.float32
    )


def add_prior(matrix, row_ids, column_ids, column_prior):
    return matrix + jnp.where(
        row_ids[:, None] == column_ids[None, :], column_prior[None, :], jnp.float32(0.0)
    )


def by_blocks(design, whitener, arc_length, gap_mask, prior_diag):
    weights = jnp.where(live_mask(arc_length, gap_mask), jnp.float32(1.0), jnp.float32(0.0))
    row_index = lax.axis_index("row")
    col_index = lax.axis_index("col")
    row_count = lax.axis_size("row")
    col_count = lax.axis_size("col")
    col_width = design.shape[1]
    strip_width = col_width // row_count
    regrouped = lax.all_to_all(design, "row", split_axis=1, concat_axis=0, tiled=True)
    own_strip = whiten_rows(regrouped, whitener, weights)
    column_side = lax.all_gather(own_strip, "row", axis=1, tiled=True)
    column_ids = col_index * col_width + lax.broadcasted_iota(jnp.int32, (col_width,), 0)
    column_prior = lax.dynamic_slice_in_dim(prior_diag, col_index * col_width, col_width)
    first_ids = lax.broadcasted_iota(jnp.int32, (PANEL,), 0)
    block_ids = lax.broadcasted_iota(jnp.int32, (col_count, strip_width), 0) * col_width
    block_ids = (
        block_ids
        + row_index * strip_width
        + lax.broadcasted_iota(jnp.int32, (col_count, strip_width), 1)
    ).reshape(-1)
    first_white = broadcast(own_strip[:, :PANEL], ("row", "col"), 0)
    top_rows = add_prior(
        contract_rows(first_white, column_side), first_ids, column_ids, column_prior
    )
    corner = add_prior(
        contract_rows(first_white, first_white), first_ids, first_ids, prior_diag[:PANEL]
    )
    section = lax.all_gather(own_strip, "col", axis=1, tiled=True)
    wide_tile = jnp.concatenate(
        [contract_rows(section, column_side), contract_rows(section, first_white)], axis=1
    )
    normal_tile = add_prior(wide_tile[:, :col_width], block_ids, column_ids, column_prior)
    panel_cols = add_prior(wide_tile[:, col_width:], block_ids, first_ids, prior_diag[:PANEL])
    factor = jnp.linalg.cholesky(corner)
    panel_left = lax.linalg.triangular_solve(
        factor, panel_cols, left_side=False, lower=True, transpose_a=True
    )
    panel_top = lax.linalg.triangular_solve(factor, top_rows, left_side=True, lower=True)
    schur = normal_tile - jnp.dot(
        panel_left, panel_top, precision=lax.Precision.HIGHEST, preferred_element_type=jnp.float32
    )
    return (
        schur.reshape(col_count, strip_width, col_width),
        panel_left.reshape(col_count, strip_width, PANEL),
    )


def on_device(design, whitener, arc_length, gap_mask, prior_diag):
    live = live_mask(arc_length, gap_mask)
    row_index = lax.axis_index("row")
    col_index = lax.axis_index("col")
    rows = lax.axis_size("row")
    cols = lax.axis_size("col")
    chips = cols // 2
    arcs, epochs = live.shape
    col_width = design.shape[1]
    width = col_width // rows
    chip = col_index // 2
    order = row_index ^ jnp.arange(rows, dtype=jnp.int32)

    def swap_row(value, mask):
        return lax.ppermute(value, "row", [(r, r ^ mask) for r in range(rows)])

    def swap_core(value):
        return lax.ppermute(value, "col", [(c, c ^ 1) for c in range(cols)])

    def shift(value, step):
        pairs = [(c, c + 2 * step) for c in range(cols) if 0 <= c + 2 * step < cols]
        return lax.ppermute(value, "col", pairs)

    def strip_of(index):
        return lax.dynamic_slice_in_dim(design, index * width, width, axis=1)

    raw = [strip_of(row_index)]
    for s in range(1, rows):
        raw.append(swap_row(strip_of(row_index ^ s), s))

    begin = design[:, :PANEL]
    begin = jnp.where(col_index == 1, swap_core(begin), begin)
    for t in range(1, chips):
        begin = jnp.where(chip == t, shift(begin, 1), begin)
    raw_first = [begin] + [swap_row(begin, s) for s in range(1, rows)]

    column_prior = lax.dynamic_slice_in_dim(
        prior_diag, col_index * col_width + row_index * width, width
    ).reshape(1, width)
    first_prior = prior_diag[:PANEL]
    table = line_schedule(chips)

    def run(sent, raw, raw_first):
        kept = -(-sent // LANES) * LANES
        mixer = compact_whitener(whitener, live, sent)
        own = whiten(order, mixer, raw)
        first = whiten(order, mixer, raw_first)

        moving = {0: own, 1: own}
        arrived = {}
        for t in range(1, chips):
            moving = {0: shift(moving[0], 1), 1: shift(moving[1], -1)}
            arrived[0, t], arrived[1, t] = moving[0], moving[1]

        core = col_index % 2

        near = [own] + [swap_row(own, 1 << b) for b in range((rows - 1).bit_length())]
        half = sent // 32 * 16
        strips = {0: [own], 1: [near[1]], 2: [near[2]]}
        strips[3] = [swap_row(near[2][:half], 1), swap_row(near[1][half:], 2)]

        inverse, inv_t = factor_inverse(first, first_prior.reshape(1, PANEL))
        wide = jnp.pad(first, ((0, kept - sent), (0, 0)))
        top_prior = first_prior.reshape(PANEL, 1)
        right = None
        for s in range(rows):
            spot = (col_index + (row_index ^ s)).reshape(1)
            right = right_side(
                kept, s, rows, spot, first, top_prior, inverse, strips[s], right
            )

        held = None
        sibling = {0: swap_core(own)}
        for key, value in arrived.items():
            sibling[key] = swap_core(value)
        for t in range(chips):
            if t == 0:
                keys, target, choice = [0], chip, jnp.int32(0)
                source = {0: own}
            else:
                wanted = [table[z][t - 1] for z in range(chips)]
                keys = sorted({(side, d) for _, side, d in wanted})
                target = jnp.asarray(np.array([q for q, _, _ in wanted], np.int32))[chip]
                choice = jnp.asarray(
                    np.array([keys.index((side, d)) for _, side, d in wanted], np.int32)
                )[chip]
                source = arrived
            pairs = [(source[k], sibling[k]) for k in keys]
            at = jnp.stack([target, row_index, col_index, choice, core]).astype(jnp.int32)
            held = tiles(
                kept, at, order, pairs, right, wide, column_prior,
                first_prior.reshape(1, PANEL), inv_t, cols, held,
            )
        return held

    most = 3 * epochs
    sizes = [most * 19 // 24, most]
    count = jnp.sum(live.astype(jnp.int32))
    return lax.switch(
        jnp.where(count <= sizes[0], 0, 1),
        [functools.partial(run, size) for size in sizes],
        raw,
        raw_first,
    )


def solution(mesh):
    def run(design, whitener, arc_length, gap_mask, prior_diag):
        rows = lax.axis_size("row")
        fits = rows == 4 and whitener.shape[0] == rows and design.shape[1] % (rows * LANES) == 0
        form = on_device if fits else by_blocks
        return form(design, whitener, arc_length, gap_mask, prior_diag)

    placed = (P("row", "col"), P(), P(), P(), P())
    return jax.shard_map(
        run,
        mesh=mesh,
        in_specs=placed,
        out_specs=(P(None, "row", "col"), P(None, "row", None)),
        check_vma=False,
    )
```
